32 devices in a mesh: grp: 2 (over x), azi: 4 (over y, core), pln: 4 (over z).
Axes of the slice: x: 2, y: 2, z: 4, core: 2. Of those that a mesh axis runs over, the one named last changes fastest.
Arguments:
- fields: float32 [5, 16, 128, 1024], P(None, 'grp', 'pln', 'azi'), parts along dimension 1, may hold values from -8 to 8
- swirl_cfl: float32 [16, 128, 1024], P('grp', 'pln', 'azi'), parts along dimension 0, may hold values from 1 to 32768
Outputs:
- advanced: float32 [5, 16, 128, 1024], P(None, 'grp', 'pln', 'azi'), parts along dimension 1
The draws below stay inside these ranges and needn't reach their ends.
There are 2 independent parts, one for each index of `grp`. The reference program is written for one: setup_inputs(seed, part) draws one part's arguments, and reference() takes and returns one part's arrays. A program takes and returns all parts, laid end to end along the dimension named above; each array names one. Nothing has to cross between parts.
All inputs are finite; a program needn't handle non-finite values.
Results may differ from the reference program's by a relative error of at most 0.000082.
Values sent between devices are 32-bit elements; how exact they have to be, the bound alone decides.
A program may use at most 64 MiB of HBM per device.

```python
import math
import jax
import jax.numpy as jnp
from jax import lax

RADIAL_PLANES = 8
TH_DEV = 256
AXIAL_CELLS = 128
AZIMUTH_CELLS = 1024


def draw_fields(key, part):
    rough_key = jax.random.fold_in(key, 11)
    level_key = jax.random.fold_in(key, 12)
    rough = jax.random.normal(rough_key, (5, RADIAL_PLANES, AXIAL_CELLS, AZIMUTH_CELLS), jnp.float32)
    level = 0.7 * jax.random.normal(level_key, (5, RADIAL_PLANES, AXIAL_CELLS, 1), jnp.float32)
    return jnp.clip(rough + level, -8.0, 8.0)


def draw_swirl_cfl(key, part):
    kind_key = jax.random.fold_in(key, 21)
    fast_key = jax.random.fold_in(key, 22)
    slow_key = jax.random.fold_in(key, 23)
    block_key = jax.random.fold_in(key, 24)
    cell_key = jax.random.fold_in(key, 25)
    pulse_key = jax.random.fold_in(key, 26)
    spot_key = jax.random.fold_in(key, 27)
    shares = 5
    slow_line = jax.random.randint(kind_key, (RADIAL_PLANES, AXIAL_CELLS, 1), 0, 10) < shares
    fast_rate = jnp.exp(jax.random.uniform(fast_key, (RADIAL_PLANES, AXIAL_CELLS, 1), jnp.float32, math.log(25.0), math.log(60.0)))
    slow_rate = jnp.exp(jax.random.uniform(slow_key, (RADIAL_PLANES, AXIAL_CELLS, 1), jnp.float32, math.log(2.0 * AZIMUTH_CELLS), math.log(8.0 * AZIMUTH_CELLS)))
    line_frequency = jnp.where(slow_line, slow_rate, fast_rate)
    block_count = AZIMUTH_CELLS // TH_DEV
    block_multiplier = jnp.exp(jax.random.uniform(block_key, (RADIAL_PLANES, AXIAL_CELLS, block_count), jnp.float32, -math.log(2.0), math.log(2.0)))
    block_multiplier = jnp.repeat(block_multiplier, TH_DEV, axis=2)
    cell_multiplier = jnp.exp(jax.random.uniform(cell_key, (RADIAL_PLANES, AXIAL_CELLS, AZIMUTH_CELLS), jnp.float32, -math.log(2.0), math.log(2.0)))
    marked_points = jax.random.randint(spot_key, (3,), 0, AZIMUTH_CELLS)
    pulse_event = jnp.any(jnp.arange(AZIMUTH_CELLS, dtype=jnp.int32)[:, None] == marked_points[None, :], axis=1)
    pulse_rate = jax.random.uniform(pulse_key, (RADIAL_PLANES, AXIAL_CELLS, AZIMUTH_CELLS), jnp.float32, 1.0, 4.0)
    return jnp.where(pulse_event[None, None, :], pulse_rate, line_frequency * block_multiplier * cell_multiplier)


def setup_inputs(seed: int = 0, part: int = 0) -> dict:
    key_of = jax.random.split(jax.random.key(seed), 3)
    own_keys = jax.random.split(jax.random.fold_in(key_of[2], part), 3)
    fields = draw_fields(jax.random.fold_in(jax.random.fold_in(key_of[2], part), 71), part)
    swirl_cfl = draw_swirl_cfl(jax.random.fold_in(jax.random.fold_in(key_of[2], part), 71), part)
    return {"fields": fields, "swirl_cfl": swirl_cfl}


INNER_A = 7.0 / 9.0
INNER_B = 1.0 / 36.0
MEAN_MACH = 0.4
SECTION_STEP = 0.25
HIGHEST = lax.Precision.HIGHEST

def compact_rows(global_idx, row_count, periodic):
    filler = jnp.zeros(global_idx.shape, jnp.float32)
    lower_diag = filler + 1.0 / 3.0
    upper_diag = filler + 1.0 / 3.0
    stencil = [filler - INNER_B, filler - INNER_A, filler, filler + INNER_A, filler + INNER_B]
    if not periodic:
        near_edge = (global_idx == 1) | (global_idx == row_count - 2)
        first_row = global_idx == 0
        final_row = global_idx == row_count - 1
        outside = (global_idx < 0) | (global_idx >= row_count)
        near_taps = (0.0, -0.75, 0.0, 0.75, 0.0)
        first_taps = (0.0, 0.0, -2.5, 2.0, 0.5)
        final_taps = (-0.5, -2.0, 2.5, 0.0, 0.0)
        lower_diag = jnp.where(near_edge, 0.25, jnp.where(first_row | outside, 0.0, jnp.where(final_row, 2.0, lower_diag)))
        upper_diag = jnp.where(near_edge, 0.25, jnp.where(final_row | outside, 0.0, jnp.where(first_row, 2.0, upper_diag)))
        stencil = [jnp.where(outside, 0.0, jnp.where(near_edge, near_taps[tap_index], jnp.where(first_row, first_taps[tap_index], jnp.where(final_row, final_taps[tap_index], stencil[tap_index])))) for tap_index in range(5)]
    return (lower_diag, upper_diag, stencil)

def compact_matrix(global_idx, row_count, periodic):
    lower_diag, upper_diag, stencil = compact_rows(global_idx, row_count, periodic)
    length = global_idx.shape[0]
    lower_diag = lower_diag.at[0].set(0.0)
    upper_diag = upper_diag.at[length - 1].set(0.0)
    row_ids = lax.broadcasted_iota(jnp.int32, (length, length), 0)
    col_ids = lax.broadcasted_iota(jnp.int32, (length, length), 1)
    explicit = jnp.zeros((length, length), jnp.float32)
    for offset in range(-2, 3):
        explicit = explicit + jnp.where(col_ids == row_ids + offset, stencil[offset + 2][:, None], 0.0)
    diagonal = jnp.ones((length,), jnp.float32)
    return lax.linalg.tridiagonal_solve(lower_diag, diagonal, upper_diag, explicit)

def reference(fields, swirl_cfl):
    radial_matrix = compact_matrix(jnp.arange(RADIAL_PLANES, dtype=jnp.int32), RADIAL_PLANES, False)
    d_radial = jnp.einsum('rs,fsxt->frxt', radial_matrix, jnp.stack([fields[2], fields[4]]), precision=HIGHEST)
    wave = 2.0 * math.pi / AZIMUTH_CELLS * jnp.arange(AZIMUTH_CELLS // 2 + 1, dtype=jnp.float32)
    symbol = (2.0 * INNER_A * jnp.sin(wave) + 2.0 * INNER_B * jnp.sin(2.0 * wave)) / (1.0 + 2.0 / 3.0 * jnp.cos(wave))
    spectrum = jnp.fft.rfft(fields[3:5], axis=-1)
    d_azim = jnp.fft.irfft(spectrum * (1j * symbol), n=AZIMUTH_CELLS, axis=-1).astype(jnp.float32)
    lower_diag, upper_diag, stencil = compact_rows(jnp.arange(AXIAL_CELLS, dtype=jnp.int32), AXIAL_CELLS, False)
    lower_diag = lower_diag.at[0].set(0.0)
    upper_diag = upper_diag.at[AXIAL_CELLS - 1].set(0.0)
    padded = jnp.pad(fields, ((0, 0), (0, 0), (2, 2), (0, 0)))
    right_side = jnp.zeros_like(fields)
    for offset in range(-2, 3):
        right_side = right_side + stencil[offset + 2][:, None] * padded[:, :, 2 + offset:2 + offset + AXIAL_CELLS]
    batch_shape = fields.shape[:3]
    d_axial = lax.linalg.tridiagonal_solve(jnp.broadcast_to(lower_diag, batch_shape), jnp.ones(batch_shape, jnp.float32), jnp.broadcast_to(upper_diag, batch_shape), right_side)
    drift_terms = MEAN_MACH * d_axial
    divergence = d_axial[1] + d_radial[0] + d_azim[0]
    tendency = jnp.stack([-drift_terms[0] - divergence, -drift_terms[1] - d_axial[4], -drift_terms[2] - d_radial[1], -drift_terms[3] - d_azim[1], -drift_terms[4] - divergence])
    sectioned = fields + SECTION_STEP * tendency
    weight = 1.0 / (1.0 + swirl_cfl)
    keep_rate = swirl_cfl * weight
    source = sectioned * weight[None]
    rates_lead = jnp.moveaxis(keep_rate, -1, 0)
    sources_lead = jnp.moveaxis(source, -1, 0)

    def combine(carried, inputs):
        rate_now, source_now = inputs
        return ((rate_now * carried[0], rate_now * carried[1] + source_now), None)
    start_maps = (jnp.ones((RADIAL_PLANES, AXIAL_CELLS), jnp.float32), jnp.zeros((5, RADIAL_PLANES, AXIAL_CELLS), jnp.float32))
    totals, unused = lax.scan(combine, start_maps, (rates_lead, sources_lead))
    start_value = totals[1] / (1.0 - totals[0])

    def advance(value_now, inputs):
        rate_now, source_now = inputs
        value_next = rate_now * value_now + source_now
        return (value_next, value_next)
    unused_last, values = lax.scan(advance, start_value, (rates_lead, sources_lead))
    return jnp.moveaxis(values, 0, -1)
```

```python
import functools

import jax
import jax.numpy as jnp
import numpy as np
from jax import lax
from jax.experimental import pallas as pl
from jax.experimental.pallas import tpu as pltpu
from jax.sharding import PartitionSpec as P

INNER_A = 7.0 / 9.0
INNER_B = 1.0 / 36.0
MEAN_MACH = 0.4
SECTION_STEP = 0.25
HIGHEST = lax.Precision.HIGHEST
MESH = pl.DeviceIdType.MESH
F32 = jnp.float32
LANES = 128
CHUNK = 16
SHIFTS = (1, 2, 4, 8, 16, 32, 64)


def line_matrices(n):
    low = np.full(n, 1.0 / 3.0)
    up = np.full(n, 1.0 / 3.0)
    right = np.zeros((n, n))
    for g in range(2, n - 2):
        right[g, g - 2 : g + 3] = (-INNER_B, -INNER_A, 0.0, INNER_A, INNER_B)
    for g in (1, n - 2):
        low[g] = up[g] = 0.25
        right[g, g - 1 : g + 2] = (-0.75, 0.0, 0.75)
    low[0], up[0], low[n - 1], up[n - 1] = 0.0, 2.0, 2.0, 0.0
    right[0, :3] = (-2.5, 2.0, 0.5)
    right[n - 1, n - 3 :] = (-0.5, -2.0, 2.5)
    both = np.concatenate([np.eye(n), right], axis=1)
    pivot = np.ones(n)
    for g in range(1, n):
        factor = low[g] / pivot[g - 1]
        pivot[g] = 1.0 - factor * up[g - 1]
        both[g] -= factor * both[g - 1]
    both[n - 1] /= pivot[n - 1]
    for g in range(n - 2, -1, -1):
        both[g] = (both[g] - up[g] * both[g + 1]) / pivot[g]
    return both[:, :n], both[:, n:]


def axial_constants(planes, cells, count, far):
    n = cells * count
    inverse, matrix = line_matrices(n)
    own = np.zeros((count, planes * cells, planes * cells))
    weights = np.zeros((count, 4 * planes, planes * cells))
    halo = np.zeros((count, planes * cells, (4 + 2 * len(far)) * planes))
    to_right, to_left = {}, {}
    for k in range(count):
        a, b = k * cells, (k + 1) * cells
        if k < count - 1:
            to_right[k] = matrix[b + 1, a:b] / inverse[b + 1, b]
        if k > 0:
            to_left[k] = matrix[a - 2, a:b] / inverse[a - 2, a - 1]
    for k in range(count):
        a, b = k * cells, (k + 1) * cells
        for p in range(planes):
            rows = slice(p * cells, (p + 1) * cells)
            own[k, rows, rows] = matrix[a:b, a:b]
            if k in to_right:
                weights[k, p, rows] = to_right[k]
                weights[k, planes + p, p * cells + cells - 1] = 1.0
            if k in to_left:
                weights[k, 2 * planes + p, rows] = to_left[k]
                weights[k, 3 * planes + p, p * cells] = 1.0
            if k > 0:
                halo[k, rows, p] = inverse[a:b, a]
                halo[k, p * cells, planes + p] = (
                    matrix[a, a - 1] - inverse[a, a] * to_right[k - 1][-1]
                )
            if k < count - 1:
                halo[k, rows, 2 * planes + p] = inverse[a:b, b - 1]
                halo[k, p * cells + cells - 1, 3 * planes + p] = (
                    matrix[b - 1, b] - inverse[b - 1, b - 1] * to_left[k + 1][0]
                )
            for j, d in enumerate(far):
                if k - d >= 0:
                    start = (k - d + 1) * cells
                    halo[k, rows, (4 + j) * planes + p] = inverse[a:b, start]
                if k + d < count:
                    end = (k + d) * cells - 1
                    halo[k, rows, (4 + len(far) + j) * planes + p] = inverse[a:b, end]
    return SECTION_STEP * own, weights, SECTION_STEP * halo


def azimuth_constants(cells, total):
    root = (np.sqrt(5.0) - 3.0) / 2.0

    def inverse(offset):
        wrapped = sum(np.power(abs(root), np.abs(offset + m * total)) for m in (-1, 0, 1))
        sign = np.where(np.abs(offset) % 2 == 1, -1.0, 1.0)
        return 3.0 / np.sqrt(5.0) * sign * wrapped

    def matrix(offset):
        inner = INNER_A * (inverse(offset + 1) - inverse(offset - 1))
        return inner + INNER_B * (inverse(offset + 2) - inverse(offset - 2))

    ids = np.arange(cells)
    own = matrix(ids[None, :] - ids[:, None])
    weights = np.zeros((16, cells))
    halo = np.zeros((16, cells))
    one = np.ones((), np.int64)
    weights[0] = matrix(1 - (ids - cells)) / inverse(one)
    weights[1, cells - 1] = 1.0
    halo[0] = inverse(ids)
    halo[1, 0] = matrix(one) - inverse(0 * one) * weights[0, cells - 1]
    weights[8] = matrix((cells - 2) - (ids + cells)) / inverse(-one)
    weights[9, 0] = 1.0
    halo[8] = inverse(ids - (cells - 1))
    halo[9, cells - 1] = matrix(-one) - inverse(0 * one) * weights[8, 0]
    return SECTION_STEP * own, weights, SECTION_STEP * halo


def dot(a, b, dims=((1,), (0,))):
    return lax.dot_general(
        a, b, (dims, ((), ())), precision=HIGHEST, preferred_element_type=F32
    )


def kernel(
    n_pln, n_azi, planes, far,
    x_hbm, c_hbm, own_hbm, w_hbm, u_hbm, az_hbm, wa_hbm, ua_hbm, ra_hbm, o_hbm,
    x, c, own, w, u, az, wa, ua, ra,
    h, ha, sb, sa, acc, rad, azd, am, acum, wt, s, g, inc, out,
    load_sem, out_sem, send_sem, recv_sem, asend_sem, arecv_sem, gsend_sem, grecv_sem,
):
    pln = lax.axis_index("pln")
    azi = lax.axis_index("azi")
    rows = x.shape[1]
    cells = x.shape[2]
    pair = 2 * planes
    steps = rows // CHUNK

    loads = []

    def load(src, dst):
        copy = pltpu.make_async_copy(src, dst, load_sem.at[len(loads)])
        copy.start()
        loads.append(copy)
        return copy

    get_w = load(w_hbm.at[pln], w)
    get_x = [load(x_hbm.at[f], x.at[f]) for f in range(5)]
    get_wa = load(wa_hbm, wa)
    get_c = load(c_hbm, c)
    get_own = load(own_hbm.at[pln], own)
    get_az = load(az_hbm, az)
    get_ra = load(ra_hbm, ra)
    get_u = load(u_hbm.at[pln], u)
    get_ua = load(ua_hbm, ua)

    h[...] = jnp.zeros_like(h)

    barrier = pltpu.get_barrier_semaphore()
    distances = (1,) + tuple(far)
    expected = jnp.int32(n_azi - 1)
    for d in distances:
        for sign in (1, -1):
            target = pln + sign * d
            valid = (target >= 0) & (target < n_pln)
            expected = expected + valid.astype(jnp.int32)

            @pl.when(valid)
            def _(target=target):
                pl.semaphore_signal(barrier, 1, device_id={"pln": target}, device_id_type=MESH)

    for d in range(1, n_azi):
        peer = lax.rem(azi + d, n_azi)
        pl.semaphore_signal(barrier, 1, device_id={"azi": peer}, device_id_type=MESH)

    get_w.wait()
    for f in range(5):
        get_x[f].wait()
        sb[f] = dot(w[...], x[f])
    pl.semaphore_wait(barrier, expected)

    transfers = []
    for sign in (1, -1):
        base = 0 if sign == 1 else pair
        for j, d in enumerate(distances):
            if d == 1:
                src = sb.at[:, pl.ds(base, pair)]
                dst = h.at[:, pl.ds(base, pair)]
            else:
                slot = 2 * pair + ((j - 1) + (0 if sign == 1 else len(far))) * planes
                src = sb.at[:, pl.ds(base, planes)]
                dst = h.at[:, pl.ds(slot, planes)]
            target = pln + sign * d
            source = pln - sign * d
            index = len(transfers)
            copy = pltpu.make_async_remote_copy(
                src_ref=src, dst_ref=dst, send_sem=send_sem.at[index],
                recv_sem=recv_sem.at[index], device_id={"pln": target}, device_id_type=MESH,
            )
            sends = (target >= 0) & (target < n_pln)
            receives = (source >= 0) & (source < n_pln)
            transfers.append((d, copy, sends, receives))
    for d, copy, sends, receives in sorted(transfers, key=lambda t: t[0]):

        @pl.when(sends)
        def _(copy=copy):
            copy.start()

    get_wa.wait()
    for f in range(2):
        sa[:, pl.ds(f * rows, rows)] = dot(wa[...], x[3 + f], ((1,), (1,)))
    around = []
    for j, step in enumerate((1, n_azi - 1)):
        copy = pltpu.make_async_remote_copy(
            src_ref=sa.at[pl.ds(8 * j, 8)], dst_ref=ha.at[pl.ds(8 * j, 8)],
            send_sem=asend_sem.at[j], recv_sem=arecv_sem.at[j],
            device_id={"azi": lax.rem(azi + step, n_azi)}, device_id_type=MESH,
        )
        copy.start()
        around.append(copy)

    get_own.wait()
    for f in range(5):
        acc[f] = dot(own[...], x[f])
    get_az.wait()
    for f in range(2):
        azd[f] = dot(x[3 + f], az[...])
    get_ra.wait()
    rad[0] = dot(ra[...], x[2])
    rad[1] = dot(ra[...], x[4])

    lane = lax.broadcasted_iota(jnp.int32, (CHUNK, LANES), 1)
    get_c.wait()

    def rate_step(it, carry):
        at = pl.ds(pl.multiple_of(it * CHUNK, CHUNK), CHUNK)
        halves = []
        for half in range(2):
            cols = pl.ds(half * LANES, LANES)
            e = 1.0 / (1.0 + c[at, cols])
            wt[at, cols] = e
            for k, shift in enumerate(SHIFTS):
                keep = jnp.where(lane >= shift, 1.0 - e, 0.0)
                am[k, at, cols] = keep
                e = e + keep * pltpu.roll(e, shift, 1)
            halves.append(e)
        first, second = halves
        acum[at, pl.ds(0, LANES)] = 1.0 - first
        am[len(SHIFTS), at, pl.ds(0, LANES)] = 1.0 - second
        second = second + (1.0 - second) * first[:, LANES - 1 :]
        acum[at, pl.ds(LANES, LANES)] = 1.0 - second
        s[5, at, pl.ds(LANES, LANES)] = second
        return carry

    lax.fori_loop(0, steps, rate_step, 0)

    get_u.wait()
    get_ua.wait()
    for copy in around:
        copy.wait_recv()
    for f in range(2):
        azd[f] += dot(ha[:, pl.ds(f * rows, rows)], ua[...], ((0,), (0,)))
    for d, copy, sends, receives in transfers:

        @pl.when(receives)
        def _(copy=copy):
            copy.wait_recv()

    for f in range(5):
        acc[f] += dot(u[...], h[f])

    def section_step(it, carry):
        at = pl.ds(pl.multiple_of(it * CHUNK, CHUNK), CHUNK)
        firsts = None
        for half in range(2):
            cols = pl.ds(half * LANES, LANES)
            ax = [acc[f, at, cols] for f in range(5)]
            div = ax[1] + rad[0, at, cols] + azd[0, at, cols]
            other = (div, ax[4], rad[1, at, cols], azd[1, at, cols], div)
            weight = wt[at, cols]
            values = [
                (x[f, at, cols] - MEAN_MACH * ax[f] - other[f]) * weight for f in range(5)
            ]
            for k, shift in enumerate(SHIFTS):
                keep = am[k, at, cols]
                values = [v + keep * pltpu.roll(v, shift, 1) for v in values]
            if half == 1:
                keep = am[len(SHIFTS), at, pl.ds(0, LANES)]
                values = [v + keep * p[:, LANES - 1 :] for v, p in zip(values, firsts)]
            for f in range(5):
                s[f, at, cols] = values[f]
            firsts = values
        return carry

    lax.fori_loop(0, steps, section_step, 0)

    sub = lax.broadcasted_iota(jnp.int32, (8, LANES), 0)
    col = lax.broadcasted_iota(jnp.int32, (8, LANES), 1)
    maps = jnp.zeros((8, rows), F32)
    for q in range(6):
        pick = jnp.where((sub == q) & (col == LANES - 1), 1.0, 0.0)
        maps = maps + dot(pick, s[q, :, pl.ds(LANES, LANES)], ((1,), (1,)))
    g[0] = maps
    gathers = []
    for d in range(1, n_azi):
        copy = pltpu.make_async_remote_copy(
            src_ref=g.at[0], dst_ref=g.at[d], send_sem=gsend_sem.at[d - 1],
            recv_sem=grecv_sem.at[d - 1],
            device_id={"azi": lax.rem(azi + d, n_azi)}, device_id_type=MESH,
        )
        copy.start()
        gathers.append(copy)
    for copy in gathers:
        copy.wait_recv()
    total = g[0]
    for d in range(n_azi - 1, 0, -1):
        block = g[d]
        total = block + (1.0 - block[5:6]) * total
    used = lax.broadcasted_iota(jnp.int32, (8, rows), 0) < 5
    incoming = jnp.where(used, total / total[5:6], 0.0)

    stores = []
    for q in range(5):
        spread = jnp.where(sub == q, 1.0, 0.0)
        inc[...] = dot(incoming, spread, ((0,), (0,)))

        def final_step(it, carry, q=q):
            at = pl.ds(pl.multiple_of(it * CHUNK, CHUNK), CHUNK)
            for half in range(2):
                cols = pl.ds(half * LANES, LANES)
                out[q, at, cols] = s[q, at, cols] + acum[at, cols] * inc[at]
            return carry

        lax.fori_loop(0, steps, final_step, 0, unroll=4)
        copy = pltpu.make_async_copy(out.at[q], o_hbm.at[q], out_sem.at[q])
        copy.start()
        stores.append(copy)

    for d, copy, sends, receives in transfers:

        @pl.when(sends)
        def _(copy=copy):
            copy.wait_send()

    for copy in around + gathers:
        copy.wait_send()
    for copy in stores:
        copy.wait()


def local(fields, swirl_cfl):
    count, planes, axial, cells = fields.shape
    n_pln = lax.axis_size("pln")
    n_azi = lax.axis_size("azi")
    rows = planes * axial
    root = (3.0 - np.sqrt(5.0)) / 2.0
    tiny = float(np.finfo(np.float32).tiny)
    far = [d for d in range(2, n_pln) if 2.0 * root ** (axial * (d - 1)) >= tiny]
    own, weights, halo = axial_constants(planes, axial, n_pln, far)
    azim, azim_weights, azim_halo = azimuth_constants(cells, cells * n_azi)
    radial = SECTION_STEP * np.kron(line_matrices(planes)[1], np.eye(axial))
    constants = [
        jnp.asarray(a, F32) for a in (own, weights, halo, azim, azim_weights, azim_halo, radial)
    ]
    halo_rows = (4 + 2 * len(far)) * planes
    ways = 2 * (1 + len(far))
    vmem = lambda *shape: pltpu.VMEM(shape, F32)
    dma = lambda size: pltpu.SemaphoreType.DMA((size,))
    out = pl.pallas_call(
        functools.partial(kernel, n_pln, n_azi, planes, far),
        out_shape=jax.ShapeDtypeStruct((5, rows, cells), F32),
        in_specs=[pl.BlockSpec(memory_space=pl.ANY)] * 9,
        out_specs=pl.BlockSpec(memory_space=pl.ANY),
        scratch_shapes=[
            vmem(5, rows, cells),
            vmem(rows, cells),
            vmem(rows, rows),
            vmem(4 * planes, rows),
            vmem(rows, halo_rows),
            vmem(cells, cells),
            vmem(16, cells),
            vmem(16, cells),
            vmem(rows, rows),
            vmem(5, halo_rows, cells),
            vmem(16, 2 * rows),
            vmem(5, 4 * planes, cells),
            vmem(16, 2 * rows),
            vmem(5, rows, cells),
            vmem(2, rows, cells),
            vmem(2, rows, cells),
            vmem(len(SHIFTS) + 1, rows, cells),
            vmem(rows, cells),
            vmem(rows, cells),
            vmem(6, rows, cells),
            vmem(n_azi, 8, rows),
            vmem(rows, LANES),
            vmem(5, rows, cells),
            dma(13),
            dma(5),
            dma(ways),
            dma(ways),
            dma(2),
            dma(2),
            dma(n_azi - 1),
            dma(n_azi - 1),
        ],
        compiler_params=pltpu.CompilerParams(
            collective_id=0, has_side_effects=True, vmem_limit_bytes=40 * 1024 * 1024
        ),
    )(fields.reshape(count, rows, cells), swirl_cfl.reshape(rows, cells), *constants)
    return out.reshape(fields.shape)


def solution(mesh):
    placed = (P(None, "grp", "pln", "azi"), P("grp", "pln", "azi"))
    return jax.shard_map(
        local, mesh=mesh, in_specs=placed, out_specs=P(None, "grp", "pln", "azi"), check_vma=False
    )
```

```python
import functools

import jax
import jax.numpy as jnp
import numpy as np
from jax import lax
from jax.experimental import pallas as pl
from jax.experimental.pallas import tpu as pltpu
from jax.sharding import PartitionSpec as P

INNER_A = 7.0 / 9.0
INNER_B = 1.0 / 36.0
MEAN_MACH = 0.4
SECTION_STEP = 0.25
THREE_PASS = lax.Precision.HIGH
MESH = pl.DeviceIdType.MESH
F32 = jnp.float32
LANES = 128
CHUNK = 64
RATE_CHUNK = 64
SHIFTS = (1, 2, 4, 8, 16, 32, 64)


def line_matrices(n):
    low = np.full(n, 1.0 / 3.0)
    up = np.full(n, 1.0 / 3.0)
    right = np.zeros((n, n))
    for g in range(2, n - 2):
        right[g, g - 2 : g + 3] = (-INNER_B, -INNER_A, 0.0, INNER_A, INNER_B)
    for g in (1, n - 2):
        low[g] = up[g] = 0.25
        right[g, g - 1 : g + 2] = (-0.75, 0.0, 0.75)
    low[0], up[0], low[n - 1], up[n - 1] = 0.0, 2.0, 2.0, 0.0
    right[0, :3] = (-2.5, 2.0, 0.5)
    right[n - 1, n - 3 :] = (-0.5, -2.0, 2.5)
    both = np.concatenate([np.eye(n), right], axis=1)
    pivot = np.ones(n)
    for g in range(1, n):
        factor = low[g] / pivot[g - 1]
        pivot[g] = 1.0 - factor * up[g - 1]
        both[g] -= factor * both[g - 1]
    both[n - 1] /= pivot[n - 1]
    for g in range(n - 2, -1, -1):
        both[g] = (both[g] - up[g] * both[g + 1]) / pivot[g]
    return both[:, :n], both[:, n:]


def axial_constants(planes, cells, count, far):
    n = cells * count
    inverse, matrix = line_matrices(n)
    own = np.zeros((count, planes * cells, planes * cells))
    weights = np.zeros((count, 4 * planes, planes * cells))
    halo = np.zeros((count, planes * cells, (4 + 2 * len(far)) * planes))
    to_right, to_left = {}, {}
    for k in range(count):
        a, b = k * cells, (k + 1) * cells
        if k < count - 1:
            to_right[k] = matrix[b + 1, a:b] / inverse[b + 1, b]
        if k > 0:
            to_left[k] = matrix[a - 2, a:b] / inverse[a - 2, a - 1]
    for k in range(count):
        a, b = k * cells, (k + 1) * cells
        for p in range(planes):
            rows = slice(p * cells, (p + 1) * cells)
            own[k, rows, rows] = matrix[a:b, a:b]
            if k in to_right:
                weights[k, p, rows] = to_right[k]
                weights[k, planes + p, p * cells + cells - 1] = 1.0
            if k in to_left:
                weights[k, 2 * planes + p, rows] = to_left[k]
                weights[k, 3 * planes + p, p * cells] = 1.0
            if k > 0:
                halo[k, rows, p] = inverse[a:b, a]
                halo[k, p * cells, planes + p] = (
                    matrix[a, a - 1] - inverse[a, a] * to_right[k - 1][-1]
                )
            if k < count - 1:
                halo[k, rows, 2 * planes + p] = inverse[a:b, b - 1]
                halo[k, p * cells + cells - 1, 3 * planes + p] = (
                    matrix[b - 1, b] - inverse[b - 1, b - 1] * to_left[k + 1][0]
                )
            for j, d in enumerate(far):
                if k - d >= 0:
                    start = (k - d + 1) * cells
                    halo[k, rows, (4 + j) * planes + p] = inverse[a:b, start]
                if k + d < count:
                    end = (k + d) * cells - 1
                    halo[k, rows, (4 + len(far) + j) * planes + p] = inverse[a:b, end]
    return SECTION_STEP * own, weights, SECTION_STEP * halo


def azimuth_constants(cells, total):
    root = (np.sqrt(5.0) - 3.0) / 2.0

    def inverse(offset):
        wrapped = sum(np.power(abs(root), np.abs(offset + m * total)) for m in (-1, 0, 1))
        sign = np.where(np.abs(offset) % 2 == 1, -1.0, 1.0)
        return 3.0 / np.sqrt(5.0) * sign * wrapped

    def matrix(offset):
        inner = INNER_A * (inverse(offset + 1) - inverse(offset - 1))
        return inner + INNER_B * (inverse(offset + 2) - inverse(offset - 2))

    ids = np.arange(cells)
    own = matrix(ids[None, :] - ids[:, None])
    weights = np.zeros((16, cells))
    halo = np.zeros((16, cells))
    one = np.ones((), np.int64)
    weights[0] = matrix(1 - (ids - cells)) / inverse(one)
    weights[1, cells - 1] = 1.0
    halo[0] = inverse(ids)
    halo[1, 0] = matrix(one) - inverse(0 * one) * weights[0, cells - 1]
    weights[8] = matrix((cells - 2) - (ids + cells)) / inverse(-one)
    weights[9, 0] = 1.0
    halo[8] = inverse(ids - (cells - 1))
    halo[9, cells - 1] = matrix(-one) - inverse(0 * one) * weights[8, 0]
    return SECTION_STEP * own, weights, SECTION_STEP * halo


def dot(a, b, dims=((1,), (0,))):
    return lax.dot_general(
        a, b, (dims, ((), ())), precision=THREE_PASS, preferred_element_type=F32
    )


def kernel(
    n_pln, n_azi, planes, far,
    x_hbm, c_hbm, own_hbm, w_hbm, u_hbm, az_hbm, wa_hbm, ua_hbm, ra_hbm, o_hbm,
    x, c, own, w, u, az, wa, ua, ra,
    h, ha, sb, sa, acc, rad, azd, am, acum, wt, s, g, inc, out,
    load_sem, out_sem, send_sem, recv_sem, asend_sem, arecv_sem, gsend_sem, grecv_sem,
):
    pln = lax.axis_index("pln")
    azi = lax.axis_index("azi")
    rows = x.shape[1]
    cells = x.shape[2]
    pair = 2 * planes
    steps = rows // CHUNK

    loads = []

    def load(src, dst):
        copy = pltpu.make_async_copy(src, dst, load_sem.at[len(loads)])
        copy.start()
        loads.append(copy)
        return copy

    get_w = load(w_hbm.at[pln], w)
    get_x = [load(x_hbm.at[f], x.at[f]) for f in range(5)]
    get_wa = load(wa_hbm, wa)
    get_c = load(c_hbm, c)
    get_own = load(own_hbm.at[pln], own)
    get_az = load(az_hbm, az)
    get_ra = load(ra_hbm, ra)
    get_u = load(u_hbm.at[pln], u)
    get_ua = load(ua_hbm, ua)

    h[...] = jnp.zeros_like(h)

    barrier = pltpu.get_barrier_semaphore()
    distances = (1,) + tuple(far)
    expected = jnp.int32(n_azi - 1)
    for d in distances:
        for sign in (1, -1):
            target = pln + sign * d
            valid = (target >= 0) & (target < n_pln)
            expected = expected + valid.astype(jnp.int32)

            @pl.when(valid)
            def _(target=target):
                pl.semaphore_signal(barrier, 1, device_id={"pln": target}, device_id_type=MESH)

    for d in range(1, n_azi):
        peer = lax.rem(azi + d, n_azi)
        pl.semaphore_signal(barrier, 1, device_id={"azi": peer}, device_id_type=MESH)

    get_w.wait()
    for f in range(5):
        get_x[f].wait()
        sb[f] = dot(w[...], x[f])
    pl.semaphore_wait(barrier, expected)

    transfers = []
    for sign in (1, -1):
        base = 0 if sign == 1 else pair
        for j, d in enumerate(distances):
            if d == 1:
                src = sb.at[:, pl.ds(base, pair)]
                dst = h.at[:, pl.ds(base, pair)]
            else:
                slot = 2 * pair + ((j - 1) + (0 if sign == 1 else len(far))) * planes
                src = sb.at[:, pl.ds(base, planes)]
                dst = h.at[:, pl.ds(slot, planes)]
            target = pln + sign * d
            source = pln - sign * d
            index = len(transfers)
            copy = pltpu.make_async_remote_copy(
                src_ref=src, dst_ref=dst, send_sem=send_sem.at[index],
                recv_sem=recv_sem.at[index], device_id={"pln": target}, device_id_type=MESH,
            )
            sends = (target >= 0) & (target < n_pln)
            receives = (source >= 0) & (source < n_pln)
            transfers.append((d, copy, sends, receives))
    for d, copy, sends, receives in sorted(transfers, key=lambda t: t[0]):

        @pl.when(sends)
        def _(copy=copy):
            copy.start()

    get_wa.wait()
    for f in range(2):
        sa[:, pl.ds(f * rows, rows)] = dot(wa[...], x[3 + f], ((1,), (1,)))
    around = []
    for j, step in enumerate((1, n_azi - 1)):
        copy = pltpu.make_async_remote_copy(
            src_ref=sa.at[pl.ds(8 * j, 8)], dst_ref=ha.at[pl.ds(8 * j, 8)],
            send_sem=asend_sem.at[j], recv_sem=arecv_sem.at[j],
            device_id={"azi": lax.rem(azi + step, n_azi)}, device_id_type=MESH,
        )
        copy.start()
        around.append(copy)

    get_own.wait()
    for f in range(5):
        acc[f] = dot(own[...], x[f])
    get_az.wait()
    for f in range(2):
        azd[f] = dot(x[3 + f], az[...])
    get_ra.wait()
    rad[0] = dot(ra[...], x[2])
    rad[1] = dot(ra[...], x[4])

    lane = lax.broadcasted_iota(jnp.int32, (RATE_CHUNK, LANES), 1)
    halves = [pl.ds(half * LANES, LANES) for half in range(2)]
    get_c.wait()

    def rate_step(it, carry):
        at = pl.ds(pl.multiple_of(it * RATE_CHUNK, RATE_CHUNK), RATE_CHUNK)
        parts = [1.0 / (1.0 + c[at, cols]) for cols in halves]
        for cols, e in zip(halves, parts):
            wt[at, cols] = e
        for k, shift in enumerate(SHIFTS):
            keeps = [jnp.where(lane >= shift, 1.0 - e, 0.0) for e in parts]
            for cols, keep in zip(halves, keeps):
                am[k, at, cols] = keep
            parts = [e + keep * pltpu.roll(e, shift, 1) for e, keep in zip(parts, keeps)]
        first, second = parts
        acum[at, halves[0]] = 1.0 - first
        am[len(SHIFTS), at, halves[0]] = 1.0 - second
        second = second + (1.0 - second) * first[:, LANES - 1 :]
        acum[at, halves[1]] = 1.0 - second
        s[5, at, halves[1]] = second
        return carry

    lax.fori_loop(0, rows // RATE_CHUNK, rate_step, 0)

    get_u.wait()
    get_ua.wait()
    for copy in around:
        copy.wait_recv()
    for f in range(2):
        azd[f] += dot(ha[:, pl.ds(f * rows, rows)], ua[...], ((0,), (0,)))
    for d, copy, sends, receives in transfers:

        @pl.when(receives)
        def _(copy=copy):
            copy.wait_recv()

    for f in range(5):
        acc[f] += dot(u[...], h[f])

    def section_step(it, carry):
        at = pl.ds(pl.multiple_of(it * CHUNK, CHUNK), CHUNK)
        parts = []
        for cols in halves:
            ax = [acc[f, at, cols] for f in range(5)]
            div = ax[1] + rad[0, at, cols] + azd[0, at, cols]
            other = (div, ax[4], rad[1, at, cols], azd[1, at, cols], div)
            weight = wt[at, cols]
            parts.append(
                [(x[f, at, cols] - MEAN_MACH * ax[f] - other[f]) * weight for f in range(5)]
            )
        for k, shift in enumerate(SHIFTS):
            parts = [
                [v + am[k, at, cols] * pltpu.roll(v, shift, 1) for v in values]
                for cols, values in zip(halves, parts)
            ]
        keep = am[len(SHIFTS), at, halves[0]]
        for f in range(5):
            s[f, at, halves[0]] = parts[0][f]
            s[f, at, halves[1]] = parts[1][f] + keep * parts[0][f][:, LANES - 1 :]
        return carry

    lax.fori_loop(0, steps, section_step, 0)

    sub = lax.broadcasted_iota(jnp.int32, (8, LANES), 0)
    col = lax.broadcasted_iota(jnp.int32, (8, LANES), 1)
    maps = jnp.zeros((8, rows), F32)
    for q in range(6):
        pick = jnp.where((sub == q) & (col == LANES - 1), 1.0, 0.0)
        maps = maps + dot(pick, s[q, :, pl.ds(LANES, LANES)], ((1,), (1,)))
    g[0] = maps
    gathers = []
    for d in range(1, n_azi):
        copy = pltpu.make_async_remote_copy(
            src_ref=g.at[0], dst_ref=g.at[d], send_sem=gsend_sem.at[d - 1],
            recv_sem=grecv_sem.at[d - 1],
            device_id={"azi": lax.rem(azi + d, n_azi)}, device_id_type=MESH,
        )
        copy.start()
        gathers.append(copy)
    for copy in gathers:
        copy.wait_recv()
    total = g[0]
    for d in range(n_azi - 1, 0, -1):
        block = g[d]
        total = block + (1.0 - block[5:6]) * total
    used = lax.broadcasted_iota(jnp.int32, (8, rows), 0) < 5
    incoming = jnp.where(used, total / total[5:6], 0.0)

    stores = []
    for q in range(5):
        spread = jnp.where(sub == q, 1.0, 0.0)
        inc[...] = dot(incoming, spread, ((0,), (0,)))

        def final_step(it, carry, q=q):
            at = pl.ds(pl.multiple_of(it * CHUNK, CHUNK), CHUNK)
            for cols in halves:
                out[q, at, cols] = s[q, at, cols] + acum[at, cols] * inc[at]
            return carry

        lax.fori_loop(0, steps, final_step, 0, unroll=2)
        copy = pltpu.make_async_copy(out.at[q], o_hbm.at[q], out_sem.at[q])
        copy.start()
        stores.append(copy)

    for d, copy, sends, receives in transfers:

        @pl.when(sends)
        def _(copy=copy):
            copy.wait_send()

    for copy in around + gathers:
        copy.wait_send()
    for copy in stores:
        copy.wait()


def local(fields, swirl_cfl):
    count, planes, axial, cells = fields.shape
    n_pln = lax.axis_size("pln")
    n_azi = lax.axis_size("azi")
    rows = planes * axial
    root = (3.0 - np.sqrt(5.0)) / 2.0
    tiny = float(np.finfo(np.float32).tiny)
    far = [d for d in range(2, n_pln) if 2.0 * root ** (axial * (d - 1)) >= tiny]
    own, weights, halo = axial_constants(planes, axial, n_pln, far)
    azim, azim_weights, azim_halo = azimuth_constants(cells, cells * n_azi)
    radial = SECTION_STEP * np.kron(line_matrices(planes)[1], np.eye(axial))
    constants = [
        jnp.asarray(a, F32) for a in (own, weights, halo, azim, azim_weights, azim_halo, radial)
    ]
    halo_rows = (4 + 2 * len(far)) * planes
    ways = 2 * (1 + len(far))
    vmem = lambda *shape: pltpu.VMEM(shape, F32)
    dma = lambda size: pltpu.SemaphoreType.DMA((size,))
    out = pl.pallas_call(
        functools.partial(kernel, n_pln, n_azi, planes, far),
        out_shape=jax.ShapeDtypeStruct((5, rows, cells), F32),
        in_specs=[pl.BlockSpec(memory_space=pl.ANY)] * 9,
        out_specs=pl.BlockSpec(memory_space=pl.ANY),
        scratch_shapes=[
            vmem(5, rows, cells),
            vmem(rows, cells),
            vmem(rows, rows),
            vmem(4 * planes, rows),
            vmem(rows, halo_rows),
            vmem(cells, cells),
            vmem(16, cells),
            vmem(16, cells),
            vmem(rows, rows),
            vmem(5, halo_rows, cells),
            vmem(16, 2 * rows),
            vmem(5, 4 * planes, cells),
            vmem(16, 2 * rows),
            vmem(5, rows, cells),
            vmem(2, rows, cells),
            vmem(2, rows, cells),
            vmem(len(SHIFTS) + 1, rows, cells),
            vmem(rows, cells),
            vmem(rows, cells),
            vmem(6, rows, cells),
            vmem(n_azi, 8, rows),
            vmem(rows, LANES),
            vmem(5, rows, cells),
            dma(13),
            dma(5),
            dma(ways),
            dma(ways),
            dma(2),
            dma(2),
            dma(n_azi - 1),
            dma(n_azi - 1),
        ],
        compiler_params=pltpu.CompilerParams(
            collective_id=0, has_side_effects=True, vmem_limit_bytes=60 * 1024 * 1024
        ),
    )(fields.reshape(count, rows, cells), swirl_cfl.reshape(rows, cells), *constants)
    return out.reshape(fields.shape)


def solution(mesh):
    placed = (P(None, "grp", "pln", "azi"), P("grp", "pln", "azi"))
    return jax.shard_map(
        local, mesh=mesh, in_specs=placed, out_specs=P(None, "grp", "pln", "azi"), check_vma=False
    )
```

```python
import functools

import jax
import jax.numpy as jnp
import numpy as np
from jax import lax
from jax.experimental import pallas as pl
from jax.experimental.pallas import tpu as pltpu
from jax.sharding import PartitionSpec as P

INNER_A = 7.0 / 9.0
INNER_B = 1.0 / 36.0
MEAN_MACH = 0.4
SECTION_STEP = 0.25
THREE_PASS = lax.Precision.HIGH
MESH = pl.DeviceIdType.MESH
F32 = jnp.float32
LANES = 128
CHUNK = 64
SHIFTS = (1, 2, 4, 8, 16, 32, 64)


def line_matrices(n):
    low = np.full(n, 1.0 / 3.0)
    up = np.full(n, 1.0 / 3.0)
    right = np.zeros((n, n))
    for g in range(2, n - 2):
        right[g, g - 2 : g + 3] = (-INNER_B, -INNER_A, 0.0, INNER_A, INNER_B)
    for g in (1, n - 2):
        low[g] = up[g] = 0.25
        right[g, g - 1 : g + 2] = (-0.75, 0.0, 0.75)
    low[0], up[0], low[n - 1], up[n - 1] = 0.0, 2.0, 2.0, 0.0
    right[0, :3] = (-2.5, 2.0, 0.5)
    right[n - 1, n - 3 :] = (-0.5, -2.0, 2.5)
    both = np.concatenate([np.eye(n), right], axis=1)
    pivot = np.ones(n)
    for g in range(1, n):
        factor = low[g] / pivot[g - 1]
        pivot[g] = 1.0 - factor * up[g - 1]
        both[g] -= factor * both[g - 1]
    both[n - 1] /= pivot[n - 1]
    for g in range(n - 2, -1, -1):
        both[g] = (both[g] - up[g] * both[g + 1]) / pivot[g]
    return both[:, :n], both[:, n:]


def axial_constants(planes, cells, count, far):
    n = cells * count
    inverse, matrix = line_matrices(n)
    own = np.zeros((count, planes * cells, planes * cells))
    weights = np.zeros((count, 4 * planes, planes * cells))
    halo = np.zeros((count, planes * cells, (4 + 2 * len(far)) * planes))
    to_right, to_left = {}, {}
    for k in range(count):
        a, b = k * cells, (k + 1) * cells
        if k < count - 1:
            to_right[k] = matrix[b + 1, a:b] / inverse[b + 1, b]
        if k > 0:
            to_left[k] = matrix[a - 2, a:b] / inverse[a - 2, a - 1]
    for k in range(count):
        a, b = k * cells, (k + 1) * cells
        for p in range(planes):
            rows = slice(p * cells, (p + 1) * cells)
            own[k, rows, rows] = matrix[a:b, a:b]
            if k in to_right:
                weights[k, p, rows] = to_right[k]
                weights[k, planes + p, p * cells + cells - 1] = 1.0
            if k in to_left:
                weights[k, 2 * planes + p, rows] = to_left[k]
                weights[k, 3 * planes + p, p * cells] = 1.0
            if k > 0:
                halo[k, rows, p] = inverse[a:b, a]
                halo[k, p * cells, planes + p] = (
                    matrix[a, a - 1] - inverse[a, a] * to_right[k - 1][-1]
                )
            if k < count - 1:
                halo[k, rows, 2 * planes + p] = inverse[a:b, b - 1]
                halo[k, p * cells + cells - 1, 3 * planes + p] = (
                    matrix[b - 1, b] - inverse[b - 1, b - 1] * to_left[k + 1][0]
                )
            for j, d in enumerate(far):
                if k - d >= 0:
                    start = (k - d + 1) * cells
                    halo[k, rows, (4 + j) * planes + p] = inverse[a:b, start]
                if k + d < count:
                    end = (k + d) * cells - 1
                    halo[k, rows, (4 + len(far) + j) * planes + p] = inverse[a:b, end]
    return SECTION_STEP * own, weights, SECTION_STEP * halo


def azimuth_constants(cells, total):
    root = (np.sqrt(5.0) - 3.0) / 2.0

    def inverse(offset):
        wrapped = sum(np.power(abs(root), np.abs(offset + m * total)) for m in (-1, 0, 1))
        sign = np.where(np.abs(offset) % 2 == 1, -1.0, 1.0)
        return 3.0 / np.sqrt(5.0) * sign * wrapped

    def matrix(offset):
        inner = INNER_A * (inverse(offset + 1) - inverse(offset - 1))
        return inner + INNER_B * (inverse(offset + 2) - inverse(offset - 2))

    ids = np.arange(cells)
    own = matrix(ids[None, :] - ids[:, None])
    weights = np.zeros((16, cells))
    halo = np.zeros((16, cells))
    one = np.ones((), np.int64)
    weights[0] = matrix(1 - (ids - cells)) / inverse(one)
    weights[1, cells - 1] = 1.0
    halo[0] = inverse(ids)
    halo[1, 0] = matrix(one) - inverse(0 * one) * weights[0, cells - 1]
    weights[8] = matrix((cells - 2) - (ids + cells)) / inverse(-one)
    weights[9, 0] = 1.0
    halo[8] = inverse(ids - (cells - 1))
    halo[9, cells - 1] = matrix(-one) - inverse(0 * one) * weights[8, 0]
    return SECTION_STEP * own, weights, SECTION_STEP * halo


def dot(a, b, dims=((1,), (0,))):
    return lax.dot_general(
        a, b, (dims, ((), ())), precision=THREE_PASS, preferred_element_type=F32
    )


def kernel(
    n_pln, n_azi, planes, far,
    x_hbm, c_hbm, own_hbm, w_hbm, u_hbm, az_hbm, wa_hbm, ua_hbm, ra_hbm, s_hbm, acum_hbm, inc_hbm,
    x, c, own, w, u, az, wa, ua, ra,
    h, ha, sb, sa, acc, rad, azd, am, acum, wt, s, g, inc,
    load_sem, out_sem, send_sem, recv_sem, asend_sem, arecv_sem, gsend_sem, grecv_sem,
):
    pln = lax.axis_index("pln")
    azi = lax.axis_index("azi")
    rows = x.shape[1]
    cells = x.shape[2]
    pair = 2 * planes
    steps = rows // CHUNK

    loads = []

    def load(src, dst):
        copy = pltpu.make_async_copy(src, dst, load_sem.at[len(loads)])
        copy.start()
        loads.append(copy)
        return copy

    get_w = load(w_hbm.at[pln], w)
    get_x = [load(x_hbm.at[f], x.at[f]) for f in range(5)]
    get_wa = load(wa_hbm, wa)
    get_c = load(c_hbm, c)
    get_own = load(own_hbm.at[pln], own)
    get_az = load(az_hbm, az)
    get_ra = load(ra_hbm, ra)
    get_u = load(u_hbm.at[pln], u)
    get_ua = load(ua_hbm, ua)

    h[...] = jnp.zeros_like(h)

    barrier = pltpu.get_barrier_semaphore()
    distances = (1,) + tuple(far)
    expected = jnp.int32(n_azi - 1)
    for d in distances:
        for sign in (1, -1):
            target = pln + sign * d
            valid = (target >= 0) & (target < n_pln)
            expected = expected + valid.astype(jnp.int32)

            @pl.when(valid)
            def _(target=target):
                pl.semaphore_signal(barrier, 1, device_id={"pln": target}, device_id_type=MESH)

    for d in range(1, n_azi):
        peer = lax.rem(azi + d, n_azi)
        pl.semaphore_signal(barrier, 1, device_id={"azi": peer}, device_id_type=MESH)

    transfers = []
    for sign in (1, -1):
        base = 0 if sign == 1 else pair
        for j, d in enumerate(distances):
            if d == 1:
                src_rows, dst_rows = pl.ds(base, pair), pl.ds(base, pair)
            else:
                slot = 2 * pair + ((j - 1) + (0 if sign == 1 else len(far))) * planes
                src_rows, dst_rows = pl.ds(base, planes), pl.ds(slot, planes)
            target = pln + sign * d
            source = pln - sign * d
            sends = (target >= 0) & (target < n_pln)
            receives = (source >= 0) & (source < n_pln)
            fields = [pl.ds(f, 1) for f in range(5)] if d == 1 else [pl.ds(0, 5)]
            copies = []
            for part in fields:
                index = sum(len(other[1]) for other in transfers) + len(copies)
                copies.append(
                    pltpu.make_async_remote_copy(
                        src_ref=sb.at[part, src_rows], dst_ref=h.at[part, dst_rows],
                        send_sem=send_sem.at[index], recv_sem=recv_sem.at[index],
                        device_id={"pln": target}, device_id_type=MESH,
                    )
                )
            transfers.append((d, copies, sends, receives))

    get_w.wait()
    for f in range(5):
        get_x[f].wait()
        sb[f] = dot(w[...], x[f])
        if f == 0:
            pl.semaphore_wait(barrier, expected)
        for d, copies, sends, receives in transfers:
            if d == 1:

                @pl.when(sends)
                def _(copies=copies, f=f):
                    copies[f].start()

    for d, copies, sends, receives in sorted(transfers, key=lambda t: t[0]):
        if d > 1:

            @pl.when(sends)
            def _(copies=copies):
                copies[0].start()

    get_wa.wait()
    for f in range(2):
        sa[:, pl.ds(f * rows, rows)] = dot(wa[...], x[3 + f], ((1,), (1,)))
    around = []
    for j, step in enumerate((1, n_azi - 1)):
        copy = pltpu.make_async_remote_copy(
            src_ref=sa.at[pl.ds(8 * j, 8)], dst_ref=ha.at[pl.ds(8 * j, 8)],
            send_sem=asend_sem.at[j], recv_sem=arecv_sem.at[j],
            device_id={"azi": lax.rem(azi + step, n_azi)}, device_id_type=MESH,
        )
        copy.start()
        around.append(copy)

    get_own.wait()
    for f in range(5):
        acc[f] = dot(own[...], x[f])
    get_az.wait()
    for f in range(2):
        azd[f] = dot(x[3 + f], az[...])
    get_ra.wait()
    rad[0] = dot(ra[...], x[2])
    rad[1] = dot(ra[...], x[4])

    lane = lax.broadcasted_iota(jnp.int32, (CHUNK, LANES), 1)
    line = lax.broadcasted_iota(jnp.int32, (CHUNK, LANES), 0)
    per_tile = LANES // CHUNK

    def note_end(it, q, values):
        tile = lax.div(it, per_tile)
        here = lane == line + CHUNK * lax.rem(it, per_tile)
        ends = jnp.where(here, jnp.broadcast_to(values[:, LANES - 1 :], here.shape), 0.0)
        g[0, tile, q : q + 1] += jnp.sum(ends, axis=0, keepdims=True)

    g[0] = jnp.zeros(g.shape[1:], F32)
    halves = [pl.ds(half * LANES, LANES) for half in range(2)]
    get_c.wait()

    def rate_step(it, carry):
        at = pl.ds(pl.multiple_of(it * CHUNK, CHUNK), CHUNK)
        parts = [1.0 / (1.0 + c[at, cols]) for cols in halves]
        for cols, e in zip(halves, parts):
            wt[at, cols] = e
        for k, shift in enumerate(SHIFTS):
            keeps = [jnp.where(lane >= shift, 1.0 - e, 0.0) for e in parts]
            for cols, keep in zip(halves, keeps):
                am[k, at, cols] = keep
            parts = [e + keep * pltpu.roll(e, shift, 1) for e, keep in zip(parts, keeps)]
        first, second = parts
        acum[at, halves[0]] = 1.0 - first
        am[len(SHIFTS), at, halves[0]] = 1.0 - second
        second = second + (1.0 - second) * first[:, LANES - 1 :]
        acum[at, halves[1]] = 1.0 - second
        note_end(it, 5, second)
        return carry

    lax.fori_loop(0, rows // CHUNK, rate_step, 0)

    put_acum = pltpu.make_async_copy(acum, acum_hbm, out_sem.at[5])
    put_acum.start()

    get_u.wait()
    get_ua.wait()
    for copy in around:
        copy.wait_recv()
    for f in range(2):
        azd[f] += dot(ha[:, pl.ds(f * rows, rows)], ua[...], ((0,), (0,)))
    for d, copies, sends, receives in transfers:

        @pl.when(receives)
        def _(copies=copies):
            for copy in copies:
                copy.wait_recv()

    for f in range(5):
        acc[f] += dot(u[...], h[f])

    def section_step(it, carry):
        at = pl.ds(pl.multiple_of(it * CHUNK, CHUNK), CHUNK)
        parts = []
        for cols in halves:
            ax = [acc[f, at, cols] for f in range(5)]
            div = ax[1] + rad[0, at, cols] + azd[0, at, cols]
            other = (div, ax[4], rad[1, at, cols], azd[1, at, cols], div)
            weight = wt[at, cols]
            parts.append(
                [(x[f, at, cols] - MEAN_MACH * ax[f] - other[f]) * weight for f in range(5)]
            )
        for k, shift in enumerate(SHIFTS):
            parts = [
                [v + am[k, at, cols] * pltpu.roll(v, shift, 1) for v in values]
                for cols, values in zip(halves, parts)
            ]
        keep = am[len(SHIFTS), at, halves[0]]
        for f in range(5):
            s[f, at, halves[0]] = parts[0][f]
            second = parts[1][f] + keep * parts[0][f][:, LANES - 1 :]
            s[f, at, halves[1]] = second
            note_end(it, f, second)
        return carry

    lax.fori_loop(0, steps, section_step, 0)

    gathers = []
    for d in range(1, n_azi):
        copy = pltpu.make_async_remote_copy(
            src_ref=g.at[0], dst_ref=g.at[d], send_sem=gsend_sem.at[d - 1],
            recv_sem=grecv_sem.at[d - 1],
            device_id={"azi": lax.rem(azi + d, n_azi)}, device_id_type=MESH,
        )
        copy.start()
        gathers.append(copy)
    stores = [put_acum]
    for f in range(5):
        copy = pltpu.make_async_copy(s.at[f], s_hbm.at[f], out_sem.at[f])
        copy.start()
        stores.append(copy)
    for copy in gathers:
        copy.wait_recv()
    total = g[0]
    for d in range(n_azi - 1, 0, -1):
        block = g[d]
        total = block + (1.0 - block[:, 5:6]) * total
    used = lax.broadcasted_iota(jnp.int32, total.shape, 1) < 5
    inc[...] = jnp.where(used, total / total[:, 5:6], 0.0)
    put_inc = pltpu.make_async_copy(inc, inc_hbm, out_sem.at[6])
    put_inc.start()

    for d, copies, sends, receives in transfers:

        @pl.when(sends)
        def _(copies=copies):
            for copy in copies:
                copy.wait_send()

    for copy in around + gathers:
        copy.wait_send()
    for copy in stores + [put_inc]:
        copy.wait()


def advance(
    s_hbm, acum_hbm, inc_hbm, o_hbm, s, acum, inc, wide, out, load_sem, out_sem
):
    loads = [
        pltpu.make_async_copy(inc_hbm, inc, load_sem.at[5]),
        pltpu.make_async_copy(acum_hbm, acum, load_sem.at[6]),
    ]
    loads += [pltpu.make_async_copy(s_hbm.at[f], s.at[f], load_sem.at[f]) for f in range(5)]
    for copy in loads:
        copy.start()
    rows = s.shape[1]
    loads[0].wait()
    sub = lax.broadcasted_iota(jnp.int32, (8, 5 * LANES), 0)
    col = lax.broadcasted_iota(jnp.int32, (8, 5 * LANES), 1)
    spread = jnp.where((col >= sub * LANES) & (col < (sub + 1) * LANES), 1.0, 0.0)
    for tile in range(rows // LANES):
        wide[pl.ds(tile * LANES, LANES)] = dot(inc[tile], spread, ((0,), (0,)))
    loads[1].wait()
    stores = []
    for f in range(5):
        loads[2 + f].wait()
        for half in range(2):
            cols = pl.ds(half * LANES, LANES)
            out[f, :, cols] = s[f, :, cols] + acum[:, cols] * wide[:, pl.ds(f * LANES, LANES)]
        copy = pltpu.make_async_copy(out.at[f], o_hbm.at[f], out_sem.at[f])
        copy.start()
        stores.append(copy)
    for copy in stores:
        copy.wait()


def local(fields, swirl_cfl):
    count, planes, axial, cells = fields.shape
    n_pln = lax.axis_size("pln")
    n_azi = lax.axis_size("azi")
    rows = planes * axial
    root = (3.0 - np.sqrt(5.0)) / 2.0
    tiny = float(np.finfo(np.float32).tiny)
    far = [d for d in range(2, n_pln) if 2.0 * root ** (axial * (d - 1)) >= tiny]
    own, weights, halo = axial_constants(planes, axial, n_pln, far)
    azim, azim_weights, azim_halo = azimuth_constants(cells, cells * n_azi)
    radial = SECTION_STEP * np.kron(line_matrices(planes)[1], np.eye(axial))
    constants = [
        jnp.asarray(a, F32) for a in (own, weights, halo, azim, azim_weights, azim_halo, radial)
    ]
    halo_rows = (4 + 2 * len(far)) * planes
    ways = 2 * (5 + len(far))
    vmem = lambda *shape: pltpu.VMEM(shape, F32)
    dma = lambda size: pltpu.SemaphoreType.DMA((size,))
    shape = lambda *sizes: jax.ShapeDtypeStruct(sizes, F32)
    tiles = rows // LANES
    anywhere = pl.BlockSpec(memory_space=pl.ANY)
    partial, rates, incoming = pl.pallas_call(
        functools.partial(kernel, n_pln, n_azi, planes, far),
        out_shape=(shape(5, rows, cells), shape(rows, cells), shape(tiles, 8, LANES)),
        in_specs=[anywhere] * 9,
        out_specs=[anywhere] * 3,
        scratch_shapes=[
            vmem(5, rows, cells),
            vmem(rows, cells),
            vmem(rows, rows),
            vmem(4 * planes, rows),
            vmem(rows, halo_rows),
            vmem(cells, cells),
            vmem(16, cells),
            vmem(16, cells),
            vmem(rows, rows),
            vmem(5, halo_rows, cells),
            vmem(16, 2 * rows),
            vmem(5, 4 * planes, cells),
            vmem(16, 2 * rows),
            vmem(5, rows, cells),
            vmem(2, rows, cells),
            vmem(2, rows, cells),
            vmem(len(SHIFTS) + 1, rows, cells),
            vmem(rows, cells),
            vmem(rows, cells),
            vmem(5, rows, cells),
            vmem(n_azi, tiles, 8, LANES),
            vmem(tiles, 8, LANES),
            dma(13),
            dma(7),
            dma(ways),
            dma(ways),
            dma(2),
            dma(2),
            dma(n_azi - 1),
            dma(n_azi - 1),
        ],
        compiler_params=pltpu.CompilerParams(
            collective_id=0, has_side_effects=True, vmem_limit_bytes=60 * 1024 * 1024
        ),
    )(fields.reshape(count, rows, cells), swirl_cfl.reshape(rows, cells), *constants)
    out = pl.pallas_call(
        advance,
        out_shape=shape(5, rows, cells),
        in_specs=[anywhere] * 3,
        out_specs=anywhere,
        scratch_shapes=[
            vmem(5, rows, cells),
            vmem(rows, cells),
            vmem(tiles, 8, LANES),
            vmem(rows, 5 * LANES),
            vmem(5, rows, cells),
            dma(7),
            dma(5),
        ],
        compiler_params=pltpu.CompilerParams(vmem_limit_bytes=60 * 1024 * 1024),
    )(partial, rates, incoming)
    return out.reshape(fields.shape)


def solution(mesh):
    placed = (P(None, "grp", "pln", "azi"), P("grp", "pln", "azi"))
    return jax.shard_map(
        local, mesh=mesh, in_specs=placed, out_specs=P(None, "grp", "pln", "azi"), check_vma=False
    )
```

```python
import functools

import jax
import jax.numpy as jnp
import numpy as np
from jax import lax
from jax.experimental import pallas as pl
from jax.experimental.pallas import tpu as pltpu
from jax.sharding import PartitionSpec as P

INNER_A = 7.0 / 9.0
INNER_B = 1.0 / 36.0
MEAN_MACH = 0.4
SECTION_STEP = 0.25
THREE_PASS = lax.Precision.HIGH
MESH = pl.DeviceIdType.MESH
F32 = jnp.float32
LANES = 128
CHUNK = 128
SHIFTS = (1, 2, 4, 8, 16, 32, 64)


def line_matrices(n):
    low = np.full(n, 1.0 / 3.0)
    up = np.full(n, 1.0 / 3.0)
    right = np.zeros((n, n))
    for g in range(2, n - 2):
        right[g, g - 2 : g + 3] = (-INNER_B, -INNER_A, 0.0, INNER_A, INNER_B)
    for g in (1, n - 2):
        low[g] = up[g] = 0.25
        right[g, g - 1 : g + 2] = (-0.75, 0.0, 0.75)
    low[0], up[0], low[n - 1], up[n - 1] = 0.0, 2.0, 2.0, 0.0
    right[0, :3] = (-2.5, 2.0, 0.5)
    right[n - 1, n - 3 :] = (-0.5, -2.0, 2.5)
    both = np.concatenate([np.eye(n), right], axis=1)
    pivot = np.ones(n)
    for g in range(1, n):
        factor = low[g] / pivot[g - 1]
        pivot[g] = 1.0 - factor * up[g - 1]
        both[g] -= factor * both[g - 1]
    both[n - 1] /= pivot[n - 1]
    for g in range(n - 2, -1, -1):
        both[g] = (both[g] - up[g] * both[g + 1]) / pivot[g]
    return both[:, :n], both[:, n:]


def axial_constants(planes, cells, count, far):
    n = cells * count
    inverse, matrix = line_matrices(n)
    own = np.zeros((count, planes * cells, planes * cells))
    weights = np.zeros((count, 4 * planes, planes * cells))
    halo = np.zeros((count, planes * cells, (4 + 2 * len(far)) * planes))
    to_right, to_left = {}, {}
    for k in range(count):
        a, b = k * cells, (k + 1) * cells
        if k < count - 1:
            to_right[k] = matrix[b + 1, a:b] / inverse[b + 1, b]
        if k > 0:
            to_left[k] = matrix[a - 2, a:b] / inverse[a - 2, a - 1]
    for k in range(count):
        a, b = k * cells, (k + 1) * cells
        for p in range(planes):
            rows = slice(p * cells, (p + 1) * cells)
            own[k, rows, rows] = matrix[a:b, a:b]
            if k in to_right:
                weights[k, p, rows] = to_right[k]
                weights[k, planes + p, p * cells + cells - 1] = 1.0
            if k in to_left:
                weights[k, 2 * planes + p, rows] = to_left[k]
                weights[k, 3 * planes + p, p * cells] = 1.0
            if k > 0:
                halo[k, rows, p] = inverse[a:b, a]
                halo[k, p * cells, planes + p] = (
                    matrix[a, a - 1] - inverse[a, a] * to_right[k - 1][-1]
                )
            if k < count - 1:
                halo[k, rows, 2 * planes + p] = inverse[a:b, b - 1]
                halo[k, p * cells + cells - 1, 3 * planes + p] = (
                    matrix[b - 1, b] - inverse[b - 1, b - 1] * to_left[k + 1][0]
                )
            for j, d in enumerate(far):
                if k - d >= 0:
                    start = (k - d + 1) * cells
                    halo[k, rows, (4 + j) * planes + p] = inverse[a:b, start]
                if k + d < count:
                    end = (k + d) * cells - 1
                    halo[k, rows, (4 + len(far) + j) * planes + p] = inverse[a:b, end]
    return SECTION_STEP * own, weights, SECTION_STEP * halo


def azimuth_constants(cells, total):
    root = (np.sqrt(5.0) - 3.0) / 2.0

    def inverse(offset):
        wrapped = sum(np.power(abs(root), np.abs(offset + m * total)) for m in (-1, 0, 1))
        sign = np.where(np.abs(offset) % 2 == 1, -1.0, 1.0)
        return 3.0 / np.sqrt(5.0) * sign * wrapped

    def matrix(offset):
        inner = INNER_A * (inverse(offset + 1) - inverse(offset - 1))
        return inner + INNER_B * (inverse(offset + 2) - inverse(offset - 2))

    ids = np.arange(cells)
    own = matrix(ids[None, :] - ids[:, None])
    weights = np.zeros((16, cells))
    halo = np.zeros((16, cells))
    one = np.ones((), np.int64)
    weights[0] = matrix(1 - (ids - cells)) / inverse(one)
    weights[1, cells - 1] = 1.0
    halo[0] = inverse(ids)
    halo[1, 0] = matrix(one) - inverse(0 * one) * weights[0, cells - 1]
    weights[8] = matrix((cells - 2) - (ids + cells)) / inverse(-one)
    weights[9, 0] = 1.0
    halo[8] = inverse(ids - (cells - 1))
    halo[9, cells - 1] = matrix(-one) - inverse(0 * one) * weights[8, 0]
    return SECTION_STEP * own, weights, SECTION_STEP * halo


def dot(a, b, dims=((1,), (0,))):
    return lax.dot_general(
        a, b, (dims, ((), ())), precision=THREE_PASS, preferred_element_type=F32
    )


def kernel(
    n_pln, n_azi, planes, far,
    x_hbm, c_hbm, own_hbm, w_hbm, u_hbm, az_hbm, wa_hbm, ua_hbm, ra_hbm, s_hbm, acum_hbm, inc_hbm,
    x, c, own, w, u, az, wa, ua, ra,
    h, ha, sb, sa, acc, rad, azd, am, acum, wt, s, g, inc,
    load_sem, out_sem, send_sem, recv_sem, asend_sem, arecv_sem, gsend_sem, grecv_sem,
):
    pln = lax.axis_index("pln")
    azi = lax.axis_index("azi")
    rows = x.shape[1]
    cells = x.shape[2]
    pair = 2 * planes
    steps = rows // CHUNK

    loads = []

    def load(src, dst):
        copy = pltpu.make_async_copy(src, dst, load_sem.at[len(loads)])
        copy.start()
        loads.append(copy)
        return copy

    get_w = load(w_hbm.at[pln], w)
    get_x = [load(x_hbm.at[f], x.at[f]) for f in range(5)]
    get_wa = load(wa_hbm, wa)
    get_c = load(c_hbm, c)
    get_own = load(own_hbm.at[pln], own)
    get_az = load(az_hbm, az)
    get_ra = load(ra_hbm, ra)
    get_u = load(u_hbm.at[pln], u)
    get_ua = load(ua_hbm, ua)

    h[...] = jnp.zeros_like(h)

    barrier = pltpu.get_barrier_semaphore()
    distances = (1,) + tuple(far)
    expected = jnp.int32(n_azi - 1)
    for d in distances:
        for sign in (1, -1):
            target = pln + sign * d
            valid = (target >= 0) & (target < n_pln)
            expected = expected + valid.astype(jnp.int32)

            @pl.when(valid)
            def _(target=target):
                pl.semaphore_signal(barrier, 1, device_id={"pln": target}, device_id_type=MESH)

    for d in range(1, n_azi):
        peer = lax.rem(azi + d, n_azi)
        pl.semaphore_signal(barrier, 1, device_id={"azi": peer}, device_id_type=MESH)

    transfers = []
    for sign in (1, -1):
        base = 0 if sign == 1 else pair
        for j, d in enumerate(distances):
            if d == 1:
                src_rows, dst_rows = pl.ds(base, pair), pl.ds(base, pair)
            else:
                slot = 2 * pair + ((j - 1) + (0 if sign == 1 else len(far))) * planes
                src_rows, dst_rows = pl.ds(base, planes), pl.ds(slot, planes)
            target = pln + sign * d
            source = pln - sign * d
            sends = (target >= 0) & (target < n_pln)
            receives = (source >= 0) & (source < n_pln)
            fields = [pl.ds(f, 1) for f in range(5)] if d == 1 else [pl.ds(0, 5)]
            copies = []
            for part in fields:
                index = sum(len(other[1]) for other in transfers) + len(copies)
                copies.append(
                    pltpu.make_async_remote_copy(
                        src_ref=sb.at[part, src_rows], dst_ref=h.at[part, dst_rows],
                        send_sem=send_sem.at[index], recv_sem=recv_sem.at[index],
                        device_id={"pln": target}, device_id_type=MESH,
                    )
                )
            transfers.append((d, copies, sends, receives))

    get_w.wait()
    for f in range(5):
        get_x[f].wait()
        sb[f] = dot(w[...], x[f])
        if f == 0:
            pl.semaphore_wait(barrier, expected)
        for d, copies, sends, receives in transfers:
            if d == 1:

                @pl.when(sends)
                def _(copies=copies, f=f):
                    copies[f].start()

    for d, copies, sends, receives in sorted(transfers, key=lambda t: t[0]):
        if d > 1:

            @pl.when(sends)
            def _(copies=copies):
                copies[0].start()

    get_wa.wait()
    for f in range(2):
        sa[:, pl.ds(f * rows, rows)] = dot(wa[...], x[3 + f], ((1,), (1,)))
    around = []
    for j, step in enumerate((1, n_azi - 1)):
        copy = pltpu.make_async_remote_copy(
            src_ref=sa.at[pl.ds(8 * j, 8)], dst_ref=ha.at[pl.ds(8 * j, 8)],
            send_sem=asend_sem.at[j], recv_sem=arecv_sem.at[j],
            device_id={"azi": lax.rem(azi + step, n_azi)}, device_id_type=MESH,
        )
        copy.start()
        around.append(copy)

    get_own.wait()
    for f in range(5):
        acc[f] = dot(own[...], x[f])
    get_az.wait()
    for f in range(2):
        azd[f] = dot(x[3 + f], az[...])
    get_ra.wait()
    rad[0] = dot(ra[...], x[2])
    rad[1] = dot(ra[...], x[4])

    lane = lax.broadcasted_iota(jnp.int32, (CHUNK, LANES), 1)
    line = lax.broadcasted_iota(jnp.int32, (CHUNK, LANES), 0)
    per_tile = LANES // CHUNK

    def note_end(it, q, values):
        tile = lax.div(it, per_tile)
        here = lane == line + CHUNK * lax.rem(it, per_tile)
        ends = jnp.where(here, jnp.broadcast_to(values[:, LANES - 1 :], here.shape), 0.0)
        g[0, tile, q : q + 1] += jnp.sum(ends, axis=0, keepdims=True)

    g[0] = jnp.zeros(g.shape[1:], F32)
    halves = [pl.ds(half * LANES, LANES) for half in range(2)]
    get_c.wait()

    def rate_step(it, carry):
        at = pl.ds(pl.multiple_of(it * CHUNK, CHUNK), CHUNK)
        parts = [1.0 / (1.0 + c[at, cols]) for cols in halves]
        for cols, e in zip(halves, parts):
            wt[at, cols] = e
        for k, shift in enumerate(SHIFTS):
            keeps = [jnp.where(lane >= shift, 1.0 - e, 0.0) for e in parts]
            for cols, keep in zip(halves, keeps):
                am[k, at, cols] = keep
            parts = [e + keep * pltpu.roll(e, shift, 1) for e, keep in zip(parts, keeps)]
        first, second = parts
        acum[at, halves[0]] = 1.0 - first
        am[len(SHIFTS), at, halves[0]] = 1.0 - second
        second = second + (1.0 - second) * first[:, LANES - 1 :]
        acum[at, halves[1]] = 1.0 - second
        note_end(it, 5, second)
        return carry

    lax.fori_loop(0, rows // CHUNK, rate_step, 0)

    put_acum = pltpu.make_async_copy(acum, acum_hbm, out_sem.at[5])
    put_acum.start()

    get_u.wait()
    get_ua.wait()
    for copy in around:
        copy.wait_recv()
    for f in range(2):
        azd[f] += dot(ha[:, pl.ds(f * rows, rows)], ua[...], ((0,), (0,)))
    for d, copies, sends, receives in transfers:

        @pl.when(receives)
        def _(copies=copies):
            for copy in copies:
                copy.wait_recv()

    for f in range(5):
        acc[f] += dot(u[...], h[f])

    def section_step(it, carry):
        at = pl.ds(pl.multiple_of(it * CHUNK, CHUNK), CHUNK)
        parts = []
        for cols in halves:
            ax = [acc[f, at, cols] for f in range(5)]
            div = ax[1] + rad[0, at, cols] + azd[0, at, cols]
            other = (div, ax[4], rad[1, at, cols], azd[1, at, cols], div)
            weight = wt[at, cols]
            parts.append(
                [(x[f, at, cols] - MEAN_MACH * ax[f] - other[f]) * weight for f in range(5)]
            )
        for k, shift in enumerate(SHIFTS):
            parts = [
                [v + am[k, at, cols] * pltpu.roll(v, shift, 1) for v in values]
                for cols, values in zip(halves, parts)
            ]
        keep = am[len(SHIFTS), at, halves[0]]
        for f in range(5):
            s[f, at, halves[0]] = parts[0][f]
            second = parts[1][f] + keep * parts[0][f][:, LANES - 1 :]
            s[f, at, halves[1]] = second
            note_end(it, f, second)
        return carry

    lax.fori_loop(0, steps, section_step, 0, unroll=2)

    gathers = []
    for d in range(1, n_azi):
        copy = pltpu.make_async_remote_copy(
            src_ref=g.at[0], dst_ref=g.at[d], send_sem=gsend_sem.at[d - 1],
            recv_sem=grecv_sem.at[d - 1],
            device_id={"azi": lax.rem(azi + d, n_azi)}, device_id_type=MESH,
        )
        copy.start()
        gathers.append(copy)
    stores = [put_acum]
    for f in range(5):
        copy = pltpu.make_async_copy(s.at[f], s_hbm.at[f], out_sem.at[f])
        copy.start()
        stores.append(copy)
    for copy in gathers:
        copy.wait_recv()
    total = g[0]
    for d in range(n_azi - 1, 0, -1):
        block = g[d]
        total = block + (1.0 - block[:, 5:6]) * total
    used = lax.broadcasted_iota(jnp.int32, total.shape, 1) < 5
    inc[...] = jnp.where(used, total / total[:, 5:6], 0.0)
    put_inc = pltpu.make_async_copy(inc, inc_hbm, out_sem.at[6])
    put_inc.start()

    for d, copies, sends, receives in transfers:

        @pl.when(sends)
        def _(copies=copies):
            for copy in copies:
                copy.wait_send()

    for copy in around + gathers:
        copy.wait_send()
    for copy in stores + [put_inc]:
        copy.wait()


def advance(
    s_hbm, acum_hbm, inc_hbm, o_hbm, s, acum, inc, wide, out, load_sem, out_sem
):
    loads = [
        pltpu.make_async_copy(inc_hbm, inc, load_sem.at[5]),
        pltpu.make_async_copy(acum_hbm, acum, load_sem.at[6]),
    ]
    loads += [pltpu.make_async_copy(s_hbm.at[f], s.at[f], load_sem.at[f]) for f in range(5)]
    for copy in loads:
        copy.start()
    rows = s.shape[1]
    loads[0].wait()
    sub = lax.broadcasted_iota(jnp.int32, (8, 5 * LANES), 0)
    col = lax.broadcasted_iota(jnp.int32, (8, 5 * LANES), 1)
    spread = jnp.where((col >= sub * LANES) & (col < (sub + 1) * LANES), 1.0, 0.0)
    for tile in range(rows // LANES):
        wide[pl.ds(tile * LANES, LANES)] = dot(inc[tile], spread, ((0,), (0,)))
    loads[1].wait()
    stores = []
    for f in range(5):
        loads[2 + f].wait()
        for half in range(2):
            cols = pl.ds(half * LANES, LANES)
            out[f, :, cols] = s[f, :, cols] + acum[:, cols] * wide[:, pl.ds(f * LANES, LANES)]
        copy = pltpu.make_async_copy(out.at[f], o_hbm.at[f], out_sem.at[f])
        copy.start()
        stores.append(copy)
    for copy in stores:
        copy.wait()


def local(fields, swirl_cfl):
    count, planes, axial, cells = fields.shape
    n_pln = lax.axis_size("pln")
    n_azi = lax.axis_size("azi")
    rows = planes * axial
    root = (3.0 - np.sqrt(5.0)) / 2.0
    tiny = float(np.finfo(np.float32).tiny)
    far = [d for d in range(2, n_pln) if 2.0 * root ** (axial * (d - 1)) >= tiny]
    own, weights, halo = axial_constants(planes, axial, n_pln, far)
    azim, azim_weights, azim_halo = azimuth_constants(cells, cells * n_azi)
    radial = SECTION_STEP * np.kron(line_matrices(planes)[1], np.eye(axial))
    constants = [
        jnp.asarray(a, F32) for a in (own, weights, halo, azim, azim_weights, azim_halo, radial)
    ]
    halo_rows = (4 + 2 * len(far)) * planes
    ways = 2 * (5 + len(far))
    vmem = lambda *shape: pltpu.VMEM(shape, F32)
    dma = lambda size: pltpu.SemaphoreType.DMA((size,))
    shape = lambda *sizes: jax.ShapeDtypeStruct(sizes, F32)
    tiles = rows // LANES
    anywhere = pl.BlockSpec(memory_space=pl.ANY)
    partial, rates, incoming = pl.pallas_call(
        functools.partial(kernel, n_pln, n_azi, planes, far),
        out_shape=(shape(5, rows, cells), shape(rows, cells), shape(tiles, 8, LANES)),
        in_specs=[anywhere] * 9,
        out_specs=[anywhere] * 3,
        scratch_shapes=[
            vmem(5, rows, cells),
            vmem(rows, cells),
            vmem(rows, rows),
            vmem(4 * planes, rows),
            vmem(rows, halo_rows),
            vmem(cells, cells),
            vmem(16, cells),
            vmem(16, cells),
            vmem(rows, rows),
            vmem(5, halo_rows, cells),
            vmem(16, 2 * rows),
            vmem(5, 4 * planes, cells),
            vmem(16, 2 * rows),
            vmem(5, rows, cells),
            vmem(2, rows, cells),
            vmem(2, rows, cells),
            vmem(len(SHIFTS) + 1, rows, cells),
            vmem(rows, cells),
            vmem(rows, cells),
            vmem(5, rows, cells),
            vmem(n_azi, tiles, 8, LANES),
            vmem(tiles, 8, LANES),
            dma(13),
            dma(7),
            dma(ways),
            dma(ways),
            dma(2),
            dma(2),
            dma(n_azi - 1),
            dma(n_azi - 1),
        ],
        compiler_params=pltpu.CompilerParams(
            collective_id=0, has_side_effects=True, vmem_limit_bytes=60 * 1024 * 1024
        ),
    )(fields.reshape(count, rows, cells), swirl_cfl.reshape(rows, cells), *constants)
    out = pl.pallas_call(
        advance,
        out_shape=shape(5, rows, cells),
        in_specs=[anywhere] * 3,
        out_specs=anywhere,
        scratch_shapes=[
            vmem(5, rows, cells),
            vmem(rows, cells),
            vmem(tiles, 8, LANES),
            vmem(rows, 5 * LANES),
            vmem(5, rows, cells),
            dma(7),
            dma(5),
        ],
        compiler_params=pltpu.CompilerParams(vmem_limit_bytes=60 * 1024 * 1024),
    )(partial, rates, incoming)
    return out.reshape(fields.shape)


def solution(mesh):
    placed = (P(None, "grp", "pln", "azi"), P("grp", "pln", "azi"))
    return jax.shard_map(
        local, mesh=mesh, in_specs=placed, out_specs=P(None, "grp", "pln", "azi"), check_vma=False
    )
```
